32 devices in a mesh: dp: 4 (over y, x), expert: 8 (over z, core).
Axes of the slice: x: 2, y: 2, z: 4, core: 2. Of those that a mesh axis runs over, the one named last changes fastest.
Arguments:
- tokens: bfloat16 [2560, 7168], P('expert', 'dp'), may hold values from -6 to 6
- route_ids: int32 [2560, 8], P('expert'), may hold values from 0 to 255, as said below
- route_scores: float32 [2560, 8], P('expert'), may hold values from 0.05 to 1
- partner: int32 [8], replicated, may hold values from 0 to 7, as said below
- w_gate: bfloat16 [8, 7168, 1024], P('expert', None, 'dp'), may hold values from -0.0625 to 0.0625
- w_up: bfloat16 [8, 7168, 1024], P('expert', None, 'dp'), may hold values from -0.0625 to 0.0625
- w_down: bfloat16 [8, 1024, 7168], P('expert', 'dp'), may hold values from -0.5 to 0.5
Outputs:
- mixed: bfloat16 [2560, 7168], P('expert', 'dp')
- placed_gate: bfloat16 [8, 7168, 1024], P('expert', None, 'dp')
- placed_up: bfloat16 [8, 7168, 1024], P('expert', None, 'dp')
- placed_down: bfloat16 [8, 1024, 7168], P('expert', 'dp')
The draws below stay inside these ranges and needn't reach their ends.
Inputs may be any that keep to these rules, and one draw needn't show every extreme that they name: `route_ids`: each token names 8 different experts, exactly one of them below 8. The 320 tokens of one index of expert name each expert below 8 at most 80 times, and one expert below 8 is named exactly 80 times by the tokens of every index. partner[e] is e or e xor 1, and partner[partner[e]] = e.
All inputs are finite; a program needn't handle non-finite values.
Results may differ from the reference program's by a relative error of at most 0.017.
Values may be sent and summed in bfloat16 or wider, within the bound.
A program may use at most 192 MiB of HBM per device.

```python
import jax
import jax.numpy as jnp
from jax import lax

D = 7168
MI = 1024
ROUTED = 256
TOP = 8
TOK_DEV = 320
EXPERTS = 8
CAP = 80
TOKENS = 2560
N_DP = 4


def draw_route_ids(key, part):
    key_full, key_pool, key_base, key_offset, key_column = jax.random.split(key, 5)
    full_expert = jax.random.randint(key_full, (), 0, EXPERTS)
    others = jnp.arange(EXPERTS - 1, dtype=jnp.int32)
    others = others + (others >= full_expert).astype(jnp.int32)
    slot_pool = jnp.repeat(others, CAP)

    def one_block(block_key):
        first_key, second_key = jax.random.split(block_key)
        chosen = jax.random.permutation(first_key, slot_pool)[:TOK_DEV - CAP]
        listed = jnp.concatenate([jnp.full((CAP,), full_expert, jnp.int32), chosen])
        return jax.random.permutation(second_key, listed)
    window_ids = jax.vmap(one_block)(jax.random.split(key_pool, EXPERTS)).reshape(TOKENS)
    span_width = ROUTED - EXPERTS
    step_width = span_width // (TOP - 1)
    base_pick = jax.random.randint(key_base, (TOKENS, 1), 0, span_width)
    offsets = jax.random.randint(key_offset, (TOKENS, TOP - 1), 0, step_width)
    outer_ids = EXPERTS + (base_pick + jnp.arange(TOP - 1, dtype=jnp.int32)[None, :] * step_width + offsets) % span_width
    window_column = jax.random.randint(key_column, (TOKENS, 1), 0, TOP)
    columns = jnp.arange(TOP, dtype=jnp.int32)[None, :]
    source_column = jnp.clip(columns - (columns > window_column).astype(jnp.int32), 0, TOP - 2)
    rest_ids = jnp.take_along_axis(outer_ids, jnp.broadcast_to(source_column, (TOKENS, TOP)), axis=1)
    return jnp.where(columns == window_column, window_ids[:, None], rest_ids).astype(jnp.int32)


def draw_partner(key, part):
    pair_flags = jax.random.randint(key, (EXPERTS // 2,), 0, 2).astype(jnp.int32)
    pair_flags = jnp.repeat(pair_flags, 2)
    return (jnp.arange(EXPERTS, dtype=jnp.int32) ^ pair_flags).astype(jnp.int32)


def shard_levels(own_key, dims, cuts, smallest, largest):
    def one(dim, parts):
        steps = jax.random.uniform(jax.random.fold_in(jax.random.fold_in(own_key, 6), dim), (parts,), jnp.float32, smallest / len(cuts), largest / len(cuts))
        return jnp.repeat(jnp.exp(steps), dims[dim] // parts).reshape((-1,) + (1,) * (len(dims) - dim - 1))

    loudness = one(*cuts[0])
    for cut in cuts[1:]:
        loudness = loudness * one(*cut)
    return loudness


def noise(own_key, extent, scale, bound, cuts=(), kind=jnp.bfloat16):
    entries = scale * jax.random.normal(own_key, extent, jnp.float32)
    if cuts:
        entries = entries * shard_levels(own_key, extent, cuts, -0.22, 0.18)
    return jnp.clip(entries, -bound, bound).astype(kind)


def setup_inputs(seed: int = 0) -> dict:
    key_of = jax.random.split(jax.random.key(seed), 8)
    tokens = noise(key_of[0], (TOKENS, D), 1.0, 6.0, ((0, 8), (1, 4)))
    route_ids = draw_route_ids(jax.random.fold_in(key_of[7], 71), 0)
    route_scores = jnp.clip(0.05 + 0.95 * jax.random.uniform(key_of[2], (TOKENS, TOP), jnp.float32) ** shard_levels(key_of[2], (TOKENS, TOP), ((0, 8),), -0.2, 0.2), 0.05, 1.0)
    partner = draw_partner(jax.random.fold_in(key_of[7], 71), 0)
    w_gate = noise(key_of[4], (EXPERTS, D, MI), D ** -0.5, 0.0625, ((0, 8), (2, 4)))
    w_up = noise(key_of[5], (EXPERTS, D, MI), D ** -0.5, 0.0625, ((0, 8), (2, 4)))
    w_down = noise(key_of[6], (EXPERTS, MI, D), (MI // 8) ** -0.5, 0.5, ((0, 8), (1, 4)))
    return {"tokens": tokens, "route_ids": route_ids, "route_scores": route_scores, "partner": partner, "w_gate": w_gate, "w_up": w_up, "w_down": w_down}


def reference(tokens, route_ids, route_scores, partner, w_gate, w_up, w_down):
    in_window = route_ids < EXPERTS
    expert_pick = jnp.sum(jnp.where(in_window, route_ids, 0), axis=1).astype(jnp.int32)
    window_score = jnp.sum(jnp.where(in_window, route_scores, jnp.zeros_like(route_scores)), axis=1)
    gate_weight = 2.5 * window_score / jnp.sum(route_scores, axis=1)
    most_rows = CAP * EXPERTS
    group_width = MI // N_DP

    def add_expert(expert_id, totals):
        chosen = expert_pick == expert_id
        picked = jnp.nonzero(chosen, size=most_rows, fill_value=0)[0].astype(jnp.int32)
        live_rows = jnp.arange(most_rows) < jnp.sum(chosen.astype(jnp.int32))
        gathered = tokens[picked]
        gate_proj = jnp.dot(gathered, w_gate[expert_id], preferred_element_type=jnp.float32)
        up_proj = jnp.dot(gathered, w_up[expert_id], preferred_element_type=jnp.float32)
        hidden = (jax.nn.silu(gate_proj) * up_proj).astype(jnp.bfloat16)
        split_hidden = hidden.reshape(most_rows, N_DP, group_width).astype(jnp.float32)
        split_down = w_down[expert_id].reshape(N_DP, group_width, D).astype(jnp.float32)
        partial_value = jnp.einsum("mqh,qhd->qmd", split_hidden, split_down).astype(jnp.bfloat16)
        combined = jnp.sum(partial_value.astype(jnp.float32), axis=0)
        combined = jnp.where(live_rows[:, None], combined, jnp.zeros_like(combined))
        return totals.at[picked].add(combined)

    totals = lax.fori_loop(0, EXPERTS, add_expert, jnp.zeros((TOKENS, D), jnp.float32))
    mixed = (gate_weight[:, None] * totals).astype(jnp.bfloat16)
    return (mixed, w_gate[partner], w_up[partner], w_down[partner])
```

```python
import functools

import jax
import jax.numpy as jnp
from jax import lax
from jax.experimental import pallas as pl
from jax.experimental.pallas import tpu as pltpu
from jax.sharding import PartitionSpec as P

MESH = pl.DeviceIdType.MESH
F32 = jnp.float32
BF16 = jnp.bfloat16


def xor(a, b, n):
    total, bit = 0, 1
    while bit < n:
        x, y = (a // bit) % 2, (b // bit) % 2
        total = total + bit * (x + y - 2 * x * y)
        bit *= 2
    return total


def dot(a, b):
    return jnp.dot(a, b, preferred_element_type=F32)


def kernel(
    E, cap, cap_pad, R,
    tokens, ids, scores, w_gate, w_up, w_down,
    mixed, sw_gate, sw_up, sw_down,
    send, tok, wgu, wd, hid, outb, ret, onehot_t, slot_row,
    w_sem, swap_send, swap_recv, wd_send, wd_recv,
    z_send, z_recv, b_send, b_recv, a_send, a_recv, f_send, f_recv, h_send, h_recv,
):
    q = lax.axis_index("dp")
    s = lax.axis_index("expert")
    qx = q + 1 - 2 * (q % 2)
    qy = (q + 2) % 4
    qd = 3 - q
    peers = (qx, qy, qd)
    T, F = tokens.shape
    H = w_gate.shape[2]
    half = (F // 256) * 128

    barrier = pltpu.get_barrier_semaphore()
    for p in peers:
        pl.semaphore_signal(barrier, inc=1, device_id=(p, s), device_id_type=MESH)

    def greet(j, _):
        pl.semaphore_signal(barrier, inc=1, device_id=(q, (s + j) % E), device_id_type=MESH)
        return 0

    lax.fori_loop(1, E, greet, 0)

    own_copies = [
        pltpu.make_async_copy(w_gate.at[0], wgu.at[:, pl.ds(0, H)], w_sem.at[0]),
        pltpu.make_async_copy(w_up.at[0], wgu.at[:, pl.ds(H, H)], w_sem.at[1]),
        pltpu.make_async_copy(
            w_down.at[0, :, pl.ds(pl.multiple_of(q * F, 128), F)], wd.at[q], w_sem.at[2]
        ),
    ]
    for c in own_copies:
        c.start()

    picks = jnp.sum(jnp.where(ids[...] < E, ids[...], 0), axis=1, keepdims=True)
    one_hot = jnp.where(
        picks == lax.broadcasted_iota(jnp.int32, (T, 128), 1), 1.0, 0.0
    ).astype(BF16)
    rows_e = max(E, 16)
    eye = jnp.where(
        lax.broadcasted_iota(jnp.int32, (rows_e, 128), 0)
        == lax.broadcasted_iota(jnp.int32, (rows_e, 128), 1), 1.0, 0.0
    ).astype(BF16)
    hot_t = lax.dot_general(
        eye, one_hot, (((1,), (1,)), ((), ())), preferred_element_type=F32
    )
    before = jnp.where(
        lax.broadcasted_iota(jnp.int32, (T, T), 0) < lax.broadcasted_iota(jnp.int32, (T, T), 1),
        1.0, 0.0,
    ).astype(BF16)
    rank_t = dot(hot_t.astype(BF16), before)
    number = lax.broadcasted_iota(jnp.int32, (rows_e, T), 0).astype(F32)
    slot_row[...] = jnp.sum(hot_t * (rank_t + number * cap_pad), axis=0, keepdims=True)
    after = jnp.where(
        lax.broadcasted_iota(jnp.int32, (T, T), 1) < lax.broadcasted_iota(jnp.int32, (T, T), 0),
        1.0, 0.0,
    ).astype(BF16)
    rank_c = jnp.sum(dot(after, one_hot) * one_hot.astype(F32), axis=1, keepdims=True)
    slot_col = rank_c + picks.astype(F32) * cap_pad
    onehot_t[...] = jnp.where(
        slot_col == lax.broadcasted_iota(jnp.int32, (T, E * cap_pad), 1).astype(F32), 1.0, 0.0
    ).astype(BF16)

    def pack(e):
        want = lax.broadcasted_iota(jnp.int32, (cap_pad, T), 0).astype(F32) + (
            e * cap_pad
        ).astype(F32)
        return dot(jnp.where(slot_row[...] == want, 1.0, 0.0).astype(BF16), tokens[...]).astype(BF16)

    pl.semaphore_wait(barrier, E + 2)

    def wd_copy(i):
        p = peers[i]
        return pltpu.make_async_remote_copy(
            w_down.at[0, :, pl.ds(pl.multiple_of(p * F, 128), F)], wd.at[q],
            wd_send.at[i], wd_recv.at[i], device_id=(p, s), device_id_type=MESH,
        )

    def swap_copy(i):
        src, dst = ((w_gate, sw_gate), (w_up, sw_up), (w_down, sw_down))[i]
        return pltpu.make_async_remote_copy(
            src, dst, swap_send.at[i], swap_recv.at[i],
            device_id=(q, s + 1 - 2 * (s % 2)), device_id_type=MESH,
        )

    def peer_of(j):
        return xor(s, (E - j) % E, E)

    def z_copy(j):
        return pltpu.make_async_remote_copy(
            send.at[j], tok.at[j, q], z_send.at[j], z_recv.at[j],
            device_id=(q, peer_of(j)), device_id_type=MESH,
        )

    def back_copy(j):
        return pltpu.make_async_remote_copy(
            outb.at[j], ret.at[pl.ds(pl.multiple_of(s * cap_pad, 16), cap_pad), :],
            b_send.at[j], b_recv.at[j],
            device_id=(q, peer_of(j)), device_id_type=MESH,
        )

    def a_copy(j, i):
        return pltpu.make_async_remote_copy(
            tok.at[j, q], tok.at[j, q], a_send.at[i, j % R], a_recv.at[i, j % R],
            device_id=(peers[i], s), device_id_type=MESH,
        )

    def f_copy(j, i):
        ref = tok.at[j, peers[1 - i], :, pl.ds(half, F - half) if i == 0 else pl.ds(0, half)]
        return pltpu.make_async_remote_copy(
            ref, ref, f_send.at[i, j % R], f_recv.at[i, j % R],
            device_id=(peers[i], s), device_id_type=MESH,
        )

    def h_copy(j, i):
        return pltpu.make_async_remote_copy(
            hid.at[j, q], hid.at[j, q], h_send.at[i, j % R], h_recv.at[i, j % R],
            device_id=(peers[i], s), device_id_type=MESH,
        )

    for i in range(3):
        wd_copy(i).start()

    def dispatch(j, _):
        send[j] = pack(peer_of(j))
        z_copy(j).start()
        return 0

    lax.fori_loop(1, E, dispatch, 0)
    tok[0, q] = pack(s)
    for i in range(3):
        swap_copy(i).start()
    for c in own_copies:
        c.wait()

    def step(t, _):
        @pl.when(t < E)
        def _():
            j = t

            @pl.when(j > 0)
            def _():
                z_copy(j).wait_recv()

            for i in range(2):
                a_copy(j, i).start()

        @pl.when((t >= 1) & (t < E + 1))
        def _():
            j = t - 1
            for i in range(2):
                a_copy(j, i).wait_recv()
            for i in range(2):
                f_copy(j, i).start()

        @pl.when((t >= 2) & (t < E + 2))
        def _():
            j = t - 2
            for i in range(2):
                f_copy(j, i).wait_recv()
            both = dot(tok[j, 0], wgu[0:F, :])
            for p in range(1, 4):
                both = both + dot(tok[j, p], wgu[p * F:(p + 1) * F, :])
            gate, up = both[:, :H], both[:, H:]
            hid[j, q] = (gate / (1.0 + jnp.exp(-gate)) * up).astype(BF16)
            for i in range(3):
                h_copy(j, i).start()

        @pl.when(t == 3)
        def _():
            for i in range(3):
                wd_copy(i).wait_recv()

        @pl.when(t >= 3)
        def _():
            j = t - 3
            for i in range(3):
                h_copy(j, i).wait_recv()

            def down(store):
                for n in range(0, F, 256):
                    acc = dot(hid[j, 0], wd[0, :, n:n + 256])
                    for p in range(1, 4):
                        acc = acc + dot(hid[j, p], wd[p, :, n:n + 256])
                    store(n, acc.astype(BF16))

            @pl.when(j == 0)
            def _():
                def store(n, v):
                    ret[pl.ds(pl.multiple_of(s * cap_pad, 16), cap_pad), n:n + 256] = v
                down(store)

            @pl.when(j > 0)
            def _():
                def store(n, v):
                    outb[j, :, n:n + 256] = v
                down(store)
                back_copy(j).start()

            for i in range(2):
                a_copy(j, i).wait_send()
                f_copy(j, i).wait_send()
            for i in range(3):
                h_copy(j, i).wait_send()

        return 0

    lax.fori_loop(0, E + 3, step, 0)

    def finish(j, _):
        z_copy(j).wait_send()
        back_copy(j).wait()
        return 0

    lax.fori_loop(1, E, finish, 0)

    inside = ids[...] < E
    weight = 2.5 * jnp.sum(jnp.where(inside, scores[...], 0.0), axis=1, keepdims=True) / jnp.sum(
        scores[...], axis=1, keepdims=True
    )
    for n in range(0, F, 256):
        mixed[:, n:n + 256] = (weight * dot(onehot_t[...], ret[:, n:n + 256])).astype(BF16)
    for i in range(3):
        wd_copy(i).wait_send()
        swap_copy(i).wait()


def body(tokens, route_ids, route_scores, partner, w_gate, w_up, w_down):
    E = lax.axis_size("expert")
    T, F = tokens.shape
    H = w_gate.shape[2]
    cap = 2 * T // E
    cap_pad = -(-cap // 16) * 16
    R = min(E, 8)
    own = lax.axis_index("expert")
    vmem = pl.BlockSpec(memory_space=pltpu.VMEM)
    hbm = pl.BlockSpec(memory_space=pl.ANY)
    dma = pltpu.SemaphoreType.DMA
    summed, sw_gate, sw_up, sw_down = pl.pallas_call(
        functools.partial(kernel, E, cap, cap_pad, R),
        out_shape=[
            jax.ShapeDtypeStruct((T, F), BF16),
            jax.ShapeDtypeStruct(w_gate.shape, BF16),
            jax.ShapeDtypeStruct(w_up.shape, BF16),
            jax.ShapeDtypeStruct(w_down.shape, BF16),
        ],
        in_specs=[vmem, vmem, vmem, hbm, hbm, hbm],
        out_specs=[vmem, hbm, hbm, hbm],
        scratch_shapes=[
            pltpu.VMEM((E, cap_pad, F), BF16),
            pltpu.VMEM((E, 4, cap_pad, F), BF16),
            pltpu.VMEM((4 * F, 2 * H), BF16),
            pltpu.VMEM((4, H, F), BF16),
            pltpu.VMEM((E, 4, cap_pad, H), BF16),
            pltpu.VMEM((E, cap_pad, F), BF16),
            pltpu.VMEM((E * cap_pad, F), BF16),
            pltpu.VMEM((T, E * cap_pad), BF16),
            pltpu.VMEM((1, T), F32),
            dma((3,)), dma((3,)), dma((3,)), dma((3,)), dma((3,)),
            dma((E,)), dma((E,)), dma((E,)), dma((E,)),
            dma((2, R)), dma((2, R)), dma((2, R)), dma((2, R)), dma((3, R)), dma((3, R)),
        ],
        compiler_params=pltpu.CompilerParams(
            collective_id=0, has_side_effects=True, vmem_limit_bytes=56 * 2**20
        ),
    )(tokens, route_ids, route_scores, w_gate, w_up, w_down)
    moved = partner[own] != own
    return (
        summed,
        jnp.where(moved, sw_gate, w_gate),
        jnp.where(moved, sw_up, w_up),
        jnp.where(moved, sw_down, w_down),
    )


def solution(mesh):
    return jax.shard_map(
        body,
        mesh=mesh,
        in_specs=(
            P("expert", "dp"),
            P("expert", None),
            P("expert", None),
            P(),
            P("expert", None, "dp"),
            P("expert", None, "dp"),
            P("expert", "dp", None),
        ),
        out_specs=(
            P("expert", "dp"),
            P("expert", None, "dp"),
            P("expert", None, "dp"),
            P("expert", "dp", None),
        ),
        check_vma=False,
    )
```

```python
import functools

import jax
import jax.numpy as jnp
from jax import lax
from jax.experimental import pallas as pl
from jax.experimental.pallas import tpu as pltpu
from jax.sharding import PartitionSpec as P

MESH = pl.DeviceIdType.MESH
F32 = jnp.float32
BF16 = jnp.bfloat16


def xor(a, b, n):
    total, bit = 0, 1
    while bit < n:
        x, y = (a // bit) % 2, (b // bit) % 2
        total = total + bit * (x + y - 2 * x * y)
        bit *= 2
    return total


def dot(a, b):
    return jnp.dot(a, b, preferred_element_type=F32)


def kernel(
    E, cap_pad, R,
    tokens_hbm, ids, scores, w_gate, w_up, w_down,
    mixed, sw_gate, sw_up, sw_down,
    tokens, send, tok, wgu, wd, hid, outb, ret, onehot_t, slot_row, weight, acc,
    t_sem, w_sem, swap_send, swap_recv, wd_send, wd_recv,
    z_send, z_recv, b_send, b_recv, a_send, a_recv, f_send, f_recv, h_send, h_recv,
):
    q = lax.axis_index("dp")
    s = lax.axis_index("expert")
    qx = q + 1 - 2 * (q % 2)
    qy = (q + 2) % 4
    qd = 3 - q
    peers = (qx, qy, qd)
    T, F = tokens.shape
    H = w_gate.shape[2]
    half = (F // 256) * 128

    barrier = pltpu.get_barrier_semaphore()
    for p in peers:
        pl.semaphore_signal(barrier, inc=1, device_id=(p, s), device_id_type=MESH)

    def greet(j, _):
        pl.semaphore_signal(barrier, inc=1, device_id=(q, (s + j) % E), device_id_type=MESH)
        return 0

    lax.fori_loop(1, E, greet, 0)

    tokens_copy = pltpu.make_async_copy(tokens_hbm, tokens, t_sem.at[0])
    tokens_copy.start()

    def wd_copy(i):
        p = peers[i]
        return pltpu.make_async_remote_copy(
            w_down.at[0, :, pl.ds(pl.multiple_of(p * F, 128), F)], wd.at[q],
            wd_send.at[i], wd_recv.at[i], device_id=(p, s), device_id_type=MESH,
        )

    def swap_copy(i):
        src, dst = ((w_gate, sw_gate), (w_up, sw_up), (w_down, sw_down))[i]
        return pltpu.make_async_remote_copy(
            src, dst, swap_send.at[i], swap_recv.at[i],
            device_id=(q, s + 1 - 2 * (s % 2)), device_id_type=MESH,
        )

    def peer_of(j):
        return xor(s, (E - j) % E, E)

    def z_copy(j):
        return pltpu.make_async_remote_copy(
            send.at[j], tok.at[j, q], z_send.at[j], z_recv.at[j],
            device_id=(q, peer_of(j)), device_id_type=MESH,
        )

    def back_copy(j):
        return pltpu.make_async_remote_copy(
            outb.at[j], ret.at[pl.ds(pl.multiple_of(s * cap_pad, 16), cap_pad), :],
            b_send.at[j], b_recv.at[j],
            device_id=(q, peer_of(j)), device_id_type=MESH,
        )

    def a_copy(j, i):
        return pltpu.make_async_remote_copy(
            tok.at[j, q], tok.at[j, q], a_send.at[i, j % R], a_recv.at[i, j % R],
            device_id=(peers[i], s), device_id_type=MESH,
        )

    def f_copy(j, i):
        ref = tok.at[j, peers[1 - i], :, pl.ds(half, F - half) if i == 0 else pl.ds(0, half)]
        return pltpu.make_async_remote_copy(
            ref, ref, f_send.at[i, j % R], f_recv.at[i, j % R],
            device_id=(peers[i], s), device_id_type=MESH,
        )

    def h_copy(j, i):
        return pltpu.make_async_remote_copy(
            hid.at[j, q], hid.at[j, q], h_send.at[i, j % R], h_recv.at[i, j % R],
            device_id=(peers[i], s), device_id_type=MESH,
        )

    own_copies = [
        pltpu.make_async_copy(
            w_down.at[0, :, pl.ds(pl.multiple_of(q * F, 128), F)], wd.at[q], w_sem.at[8]
        )
    ]
    for p in range(4):
        for i, w in enumerate((w_gate, w_up)):
            own_copies.append(pltpu.make_async_copy(
                w.at[0, pl.ds(p * F, F), :], wgu.at[p, :, pl.ds(i * H, H)], w_sem.at[2 * p + i]
            ))

    pl.semaphore_wait(barrier, E + 2)
    for i in range(3):
        wd_copy(i).start()

    inside = ids[...] < E
    picks = jnp.sum(jnp.where(inside, ids[...], 0), axis=0, keepdims=True)
    rows_e = max(E, 16)
    number = lax.broadcasted_iota(jnp.int32, (rows_e, T), 0)
    hot = jnp.where(picks == number, 1.0, 0.0)
    row_of = lax.broadcasted_iota(jnp.int32, (T, T), 0)
    col_of = lax.broadcasted_iota(jnp.int32, (T, T), 1)
    before = jnp.where(row_of < col_of, 1.0, 0.0).astype(BF16)
    rank = jnp.sum(hot * dot(hot.astype(BF16), before), axis=0, keepdims=True)
    picks_f = picks.astype(F32)
    slot_row[...] = picks_f * cap_pad + rank

    def pack(e):
        want = lax.broadcasted_iota(jnp.int32, (cap_pad, T), 0).astype(F32) + (
            e * cap_pad
        ).astype(F32)
        return dot(jnp.where(slot_row[...] == want, 1.0, 0.0).astype(BF16), tokens[...]).astype(BF16)

    tokens_copy.wait()

    def dispatch(j, _):
        send[j] = pack(peer_of(j))
        z_copy(j).start()
        return 0

    lax.fori_loop(1, E, dispatch, 0)
    tok[0, q] = pack(s)
    for i in range(2):
        a_copy(0, i).start()
    for c in own_copies:
        c.start()
    for i in range(3):
        swap_copy(i).start()

    gate_weight = 2.5 * jnp.sum(jnp.where(inside, scores[...], 0.0), axis=0, keepdims=True) / jnp.sum(
        scores[...], axis=0, keepdims=True
    )
    high = gate_weight.astype(BF16).astype(F32)
    middle = (gate_weight - high).astype(BF16).astype(F32)
    low = gate_weight - high - middle
    line = lax.broadcasted_iota(jnp.int32, (16, T), 0)
    stack = jnp.zeros((16, T), F32)
    for i, v in enumerate((picks_f, rank, high, middle, low)):
        stack = jnp.where(line == i, v, stack)
    eye = jnp.where(row_of == col_of, 1.0, 0.0).astype(BF16)
    turned = lax.dot_general(
        eye, stack.astype(BF16), (((1,), (1,)), ((), ())), preferred_element_type=F32
    )
    slot_col = turned[:, 0:1] * cap_pad + turned[:, 1:2]
    weight[...] = jnp.broadcast_to(turned[:, 2:3] + turned[:, 3:4] + turned[:, 4:5], weight.shape)
    onehot_t[...] = jnp.where(
        slot_col == lax.broadcasted_iota(jnp.int32, (T, E * cap_pad), 1).astype(F32), 1.0, 0.0
    ).astype(BF16)

    z_copy(1).wait_recv()
    for i in range(2):
        a_copy(1, i).start()
    for c in own_copies:
        c.wait()

    def step(t, _):
        @pl.when(t < E)
        def _():
            for i in range(2):
                a_copy(t, i).wait_recv()
            for i in range(2):
                f_copy(t, i).start()

        @pl.when(t + 2 < E)
        def _():
            z_copy(t + 2).wait_recv()
            for i in range(2):
                a_copy(t + 2, i).start()

        @pl.when(t < E)
        def _():
            acc[...] = (
                dot(tok[t, q], wgu[q]) + dot(tok[t, qx], wgu[qx]) + dot(tok[t, qy], wgu[qy])
            )

        @pl.when(t == 1)
        def _():
            for i in range(3):
                wd_copy(i).wait_recv()

        @pl.when(t >= 1)
        def _():
            j = t - 1
            for i in range(3):
                h_copy(j, i).wait_recv()

            def down(store):
                for n in range(0, F, 256):
                    out = dot(hid[j, 0], wd[0, :, n:n + 256])
                    for p in range(1, 4):
                        out = out + dot(hid[j, p], wd[p, :, n:n + 256])
                    store(n, out.astype(BF16))

            @pl.when(j == 0)
            def _():
                def store(n, v):
                    ret[pl.ds(pl.multiple_of(s * cap_pad, 16), cap_pad), n:n + 256] = v
                down(store)

            @pl.when(j > 0)
            def _():
                def store(n, v):
                    outb[j, :, n:n + 256] = v
                down(store)
                back_copy(j).start()

            for i in range(2):
                a_copy(j, i).wait_send()
                f_copy(j, i).wait_send()
            for i in range(3):
                h_copy(j, i).wait_send()

        @pl.when(t < E)
        def _():
            for i in range(2):
                f_copy(t, i).wait_recv()
            both = acc[...] + dot(tok[t, qd], wgu[qd])
            gate, up = both[:, :H], both[:, H:]
            hid[t, q] = (gate / (1.0 + jnp.exp(-gate)) * up).astype(BF16)
            for i in range(3):
                h_copy(t, i).start()

        return 0

    lax.fori_loop(0, E + 1, step, 0)

    def finish(j, _):
        z_copy(j).wait_send()
        back_copy(j).wait()
        return 0

    lax.fori_loop(1, E, finish, 0)
    for n in range(0, F, 256):
        mixed[:, n:n + 256] = (weight[:, :1] * dot(onehot_t[...], ret[:, n:n + 256])).astype(BF16)
    for i in range(3):
        wd_copy(i).wait_send()
        swap_copy(i).wait()


PIECES = 4


def place_kernel(partner, *refs):
    sources, targets, sem = (refs[0:3], refs[3:6]), refs[6:9], refs[9]
    own = lax.axis_index("expert")
    moved = partner[own] != own

    def pieces(group):
        for i in range(3):
            rows = group[i].shape[1] // PIECES
            for n in range(PIECES):
                cut = (0, pl.ds(n * rows, rows))
                yield pltpu.make_async_copy(
                    group[i].at[cut], targets[i].at[cut], sem.at[i * PIECES + n]
                )

    @pl.when(moved)
    def _():
        for c in pieces(sources[1]):
            c.start()

    @pl.when(jnp.logical_not(moved))
    def _():
        for c in pieces(sources[0]):
            c.start()

    for c in pieces(sources[0]):
        c.wait()


def body(tokens, route_ids, route_scores, partner, w_gate, w_up, w_down):
    E = lax.axis_size("expert")
    T, F = tokens.shape
    H = w_gate.shape[2]
    cap = 2 * T // E
    cap_pad = -(-cap // 16) * 16
    R = min(E, 8)
    vmem = pl.BlockSpec(memory_space=pltpu.VMEM)
    hbm = pl.BlockSpec(memory_space=pl.ANY)
    dma = pltpu.SemaphoreType.DMA
    weights = (w_gate, w_up, w_down)
    weight_shapes = [jax.ShapeDtypeStruct(w.shape, BF16) for w in weights]
    summed, *swapped = pl.pallas_call(
        functools.partial(kernel, E, cap_pad, R),
        out_shape=[jax.ShapeDtypeStruct((T, F), BF16)] + weight_shapes,
        in_specs=[hbm, vmem, vmem, hbm, hbm, hbm],
        out_specs=[vmem, hbm, hbm, hbm],
        scratch_shapes=[
            pltpu.VMEM((T, F), BF16),
            pltpu.VMEM((E, cap_pad, F), BF16),
            pltpu.VMEM((E, 4, cap_pad, F), BF16),
            pltpu.VMEM((4, F, 2 * H), BF16),
            pltpu.VMEM((4, H, F), BF16),
            pltpu.VMEM((E, 4, cap_pad, H), BF16),
            pltpu.VMEM((E, cap_pad, F), BF16),
            pltpu.VMEM((E * cap_pad, F), BF16),
            pltpu.VMEM((T, E * cap_pad), BF16),
            pltpu.VMEM((1, T), F32),
            pltpu.VMEM((T, 128), F32),
            pltpu.VMEM((cap_pad, 2 * H), F32),
            dma((1,)), dma((9,)), dma((3,)), dma((3,)), dma((3,)), dma((3,)),
            dma((E,)), dma((E,)), dma((E,)), dma((E,)),
            dma((2, R)), dma((2, R)), dma((2, R)), dma((2, R)), dma((3, R)), dma((3, R)),
        ],
        compiler_params=pltpu.CompilerParams(
            collective_id=0, has_side_effects=True, vmem_limit_bytes=56 * 2**20
        ),
    )(tokens, route_ids.T, route_scores.T, *weights)
    placed = pl.pallas_call(
        place_kernel,
        out_shape=weight_shapes,
        in_specs=[pl.BlockSpec(memory_space=pltpu.SMEM)] + [hbm] * 6,
        out_specs=[hbm] * 3,
        scratch_shapes=[dma((3 * PIECES,))],
        compiler_params=pltpu.CompilerParams(has_side_effects=True, vmem_limit_bytes=56 * 2**20),
    )(partner, *weights, *swapped)
    return (summed, *placed)


def solution(mesh):
    return jax.shard_map(
        body,
        mesh=mesh,
        in_specs=(
            P("expert", "dp"),
            P("expert", None),
            P("expert", None),
            P(),
            P("expert", None, "dp"),
            P("expert", None, "dp"),
            P("expert", "dp", None),
        ),
        out_specs=(
            P("expert", "dp"),
            P("expert", None, "dp"),
            P("expert", None, "dp"),
            P("expert", "dp", None),
        ),
        check_vma=False,
    )
```

```python
import functools

import jax
import jax.numpy as jnp
from jax import lax
from jax.experimental import pallas as pl
from jax.experimental.pallas import tpu as pltpu
from jax.sharding import PartitionSpec as P

MESH = pl.DeviceIdType.MESH
F32 = jnp.float32
BF16 = jnp.bfloat16


def xor(a, b, n):
    total, bit = 0, 1
    while bit < n:
        x, y = (a // bit) % 2, (b // bit) % 2
        total = total + bit * (x + y - 2 * x * y)
        bit *= 2
    return total


def dot(a, b):
    return jnp.dot(a, b, preferred_element_type=F32)


def kernel(
    E, cap_pad, R,
    tokens_hbm, ids, scores, w_gate, w_up, w_down,
    mixed, sw_gate, sw_up, sw_down,
    tokens, send, tok, wgu, wd, hid, outb, ret, onehot_t, slot_row, weight, acc,
    t_sem, w_sem, swap_send, swap_recv, wd_send, wd_recv,
    z_send, z_recv, b_send, b_recv, a_send, a_recv, f_send, f_recv, h_send, h_recv,
):
    q = lax.axis_index("dp")
    s = lax.axis_index("expert")
    qx = q + 1 - 2 * (q % 2)
    qy = (q + 2) % 4
    qd = 3 - q
    peers = (qx, qy, qd)
    T, F = tokens.shape
    H = w_gate.shape[2]
    half = (F // 256) * 128

    barrier = pltpu.get_barrier_semaphore()
    for p in peers:
        pl.semaphore_signal(barrier, inc=1, device_id=(p, s), device_id_type=MESH)

    def greet(j, _):
        pl.semaphore_signal(barrier, inc=1, device_id=(q, (s + j) % E), device_id_type=MESH)
        return 0

    lax.fori_loop(1, E, greet, 0)

    tokens_copy = pltpu.make_async_copy(tokens_hbm, tokens, t_sem.at[0])
    tokens_copy.start()

    def wd_copy(i):
        p = peers[i]
        return pltpu.make_async_remote_copy(
            w_down.at[0, :, pl.ds(pl.multiple_of(p * F, 128), F)], wd.at[q],
            wd_send.at[i], wd_recv.at[i], device_id=(p, s), device_id_type=MESH,
        )

    def swap_copy(i):
        src, dst = ((w_gate, sw_gate), (w_up, sw_up), (w_down, sw_down))[i // PIECES]
        rows = src.shape[1] // PIECES
        cut = (0, pl.ds(i % PIECES * rows, rows))
        return pltpu.make_async_remote_copy(
            src.at[cut], dst.at[cut], swap_send.at[i], swap_recv.at[i],
            device_id=(q, s + 1 - 2 * (s % 2)), device_id_type=MESH,
        )

    def peer_of(j):
        low = (E + 1 - j) // E
        return xor(s, low * j + (1 - low) * (E + 1 - j), E)

    def z_copy(j):
        return pltpu.make_async_remote_copy(
            send.at[j], tok.at[j, q], z_send.at[j], z_recv.at[j],
            device_id=(q, peer_of(j)), device_id_type=MESH,
        )

    def back_copy(j):
        return pltpu.make_async_remote_copy(
            outb.at[j], ret.at[pl.ds(pl.multiple_of(s * cap_pad, 16), cap_pad), :],
            b_send.at[j], b_recv.at[j],
            device_id=(q, peer_of(j)), device_id_type=MESH,
        )

    def a_copy(j, i):
        return pltpu.make_async_remote_copy(
            tok.at[j, q], tok.at[j, q], a_send.at[i, j % R], a_recv.at[i, j % R],
            device_id=(peers[i], s), device_id_type=MESH,
        )

    def f_copy(j, i):
        ref = tok.at[j, peers[1 - i], :, pl.ds(half, F - half) if i == 0 else pl.ds(0, half)]
        return pltpu.make_async_remote_copy(
            ref, ref, f_send.at[i, j % R], f_recv.at[i, j % R],
            device_id=(peers[i], s), device_id_type=MESH,
        )

    def h_copy(j, i):
        return pltpu.make_async_remote_copy(
            hid.at[j, q], hid.at[j, q], h_send.at[i, j % R], h_recv.at[i, j % R],
            device_id=(peers[i], s), device_id_type=MESH,
        )

    own_copies = [
        pltpu.make_async_copy(
            w_down.at[0, :, pl.ds(pl.multiple_of(q * F, 128), F)], wd.at[q], w_sem.at[8]
        )
    ]
    for p in range(4):
        for i, w in enumerate((w_gate, w_up)):
            own_copies.append(pltpu.make_async_copy(
                w.at[0, pl.ds(p * F, F), :], wgu.at[p, :, pl.ds(i * H, H)], w_sem.at[2 * p + i]
            ))

    pl.semaphore_wait(barrier, E + 2)
    for i in range(3):
        wd_copy(i).start()
    for i in range(3 * PIECES):
        swap_copy(i).start()

    inside = ids[...] < E
    picks = jnp.sum(jnp.where(inside, ids[...], 0), axis=0, keepdims=True)
    rows_e = max(E, 16)
    number = lax.broadcasted_iota(jnp.int32, (rows_e, T), 0)
    hot = jnp.where(picks == number, 1.0, 0.0)
    row_of = lax.broadcasted_iota(jnp.int32, (T, T), 0)
    col_of = lax.broadcasted_iota(jnp.int32, (T, T), 1)
    before = jnp.where(row_of < col_of, 1.0, 0.0).astype(BF16)
    rank = jnp.sum(hot * dot(hot.astype(BF16), before), axis=0, keepdims=True)
    picks_f = picks.astype(F32)
    slot_row[...] = picks_f * cap_pad + rank

    def pack(e):
        want = lax.broadcasted_iota(jnp.int32, (cap_pad, T), 0).astype(F32) + (
            e * cap_pad
        ).astype(F32)
        return dot(jnp.where(slot_row[...] == want, 1.0, 0.0).astype(BF16), tokens[...]).astype(BF16)

    tokens_copy.wait()

    def dispatch(j, _):
        send[j] = pack(peer_of(j))
        z_copy(j).start()
        return 0

    lax.fori_loop(1, E, dispatch, 0)
    tok[0, q] = pack(s)
    for i in range(2):
        a_copy(0, i).start()
    for c in own_copies:
        c.start()

    gate_weight = 2.5 * jnp.sum(jnp.where(inside, scores[...], 0.0), axis=0, keepdims=True) / jnp.sum(
        scores[...], axis=0, keepdims=True
    )
    high = gate_weight.astype(BF16).astype(F32)
    middle = (gate_weight - high).astype(BF16).astype(F32)
    low = gate_weight - high - middle
    line = lax.broadcasted_iota(jnp.int32, (16, T), 0)
    stack = jnp.zeros((16, T), F32)
    for i, v in enumerate((picks_f, rank, high, middle, low)):
        stack = jnp.where(line == i, v, stack)
    eye = jnp.where(row_of == col_of, 1.0, 0.0).astype(BF16)
    turned = lax.dot_general(
        eye, stack.astype(BF16), (((1,), (1,)), ((), ())), preferred_element_type=F32
    )
    slot_col = turned[:, 0:1] * cap_pad + turned[:, 1:2]
    weight[...] = jnp.broadcast_to(turned[:, 2:3] + turned[:, 3:4] + turned[:, 4:5], weight.shape)
    onehot_t[...] = jnp.where(
        slot_col == lax.broadcasted_iota(jnp.int32, (T, E * cap_pad), 1).astype(F32), 1.0, 0.0
    ).astype(BF16)

    z_copy(1).wait_recv()
    for i in range(2):
        a_copy(1, i).start()
    for c in own_copies:
        c.wait()

    def step(t, _):
        @pl.when(t < E)
        def _():
            for i in range(2):
                a_copy(t, i).wait_recv()
            for i in range(2):
                f_copy(t, i).start()

        @pl.when(t + 2 < E)
        def _():
            z_copy(t + 2).wait_recv()
            for i in range(2):
                a_copy(t + 2, i).start()

        @pl.when(t < E)
        def _():
            acc[...] = (
                dot(tok[t, q], wgu[q]) + dot(tok[t, qx], wgu[qx]) + dot(tok[t, qy], wgu[qy])
            )

        @pl.when(t == 1)
        def _():
            for i in range(3):
                wd_copy(i).wait_recv()

        @pl.when(t >= 1)
        def _():
            j = t - 1
            for i in range(3):
                h_copy(j, i).wait_recv()

            def down(store):
                for n in range(0, F, 256):
                    out = dot(hid[j, 0], wd[0, :, n:n + 256])
                    for p in range(1, 4):
                        out = out + dot(hid[j, p], wd[p, :, n:n + 256])
                    store(n, out.astype(BF16))

            @pl.when(j == 0)
            def _():
                def store(n, v):
                    ret[pl.ds(pl.multiple_of(s * cap_pad, 16), cap_pad), n:n + 256] = v
                down(store)

            @pl.when(j > 0)
            def _():
                def store(n, v):
                    outb[j, :, n:n + 256] = v
                down(store)
                back_copy(j).start()

            for i in range(2):
                a_copy(j, i).wait_send()
                f_copy(j, i).wait_send()
            for i in range(3):
                h_copy(j, i).wait_send()

        @pl.when(t < E)
        def _():
            for i in range(2):
                f_copy(t, i).wait_recv()
            both = acc[...] + dot(tok[t, qd], wgu[qd])
            gate, up = both[:, :H], both[:, H:]
            hid[t, q] = (gate / (1.0 + jnp.exp(-gate)) * up).astype(BF16)
            for i in range(3):
                h_copy(t, i).start()

        return 0

    lax.fori_loop(0, E + 1, step, 0)

    def finish(j, _):
        z_copy(j).wait_send()
        back_copy(j).wait()
        return 0

    lax.fori_loop(1, E, finish, 0)
    for n in range(0, F, 256):
        mixed[:, n:n + 256] = (weight[:, :1] * dot(onehot_t[...], ret[:, n:n + 256])).astype(BF16)
    for i in range(3):
        wd_copy(i).wait_send()
    for i in range(3 * PIECES):
        swap_copy(i).wait()


PIECES = 4


def place_kernel(partner, *refs):
    summed, own_set, other_set = refs[0], refs[1:4], refs[4:7]
    mixed, targets = refs[7], refs[8:11]
    rows_held, held, in_sem, out_sem = refs[11], refs[12:15], refs[15], refs[16]
    own = lax.axis_index("expert")
    moved = partner[own] != own

    def loads(group):
        for i in range(3):
            rows = group[i].shape[1] // PIECES
            for n in range(PIECES):
                cut = (0, pl.ds(n * rows, rows))
                yield (
                    pltpu.make_async_copy(
                        group[i].at[cut], held[i].at[cut], in_sem.at[i * PIECES + n]
                    ),
                    pltpu.make_async_copy(
                        held[i].at[cut], targets[i].at[cut], out_sem.at[i * PIECES + n]
                    ),
                )

    @pl.when(moved)
    def _():
        for load, _ in loads(other_set):
            load.start()

    @pl.when(jnp.logical_not(moved))
    def _():
        for load, _ in loads(own_set):
            load.start()

    sum_load = pltpu.make_async_copy(summed, rows_held, in_sem.at[3 * PIECES])
    sum_store = pltpu.make_async_copy(rows_held, mixed, out_sem.at[3 * PIECES])
    sum_load.start()
    for load, store in loads(own_set):
        load.wait()
        store.start()
    sum_load.wait()
    sum_store.start()
    for _, store in loads(own_set):
        store.wait()
    sum_store.wait()


def body(tokens, route_ids, route_scores, partner, w_gate, w_up, w_down):
    E = lax.axis_size("expert")
    T, F = tokens.shape
    H = w_gate.shape[2]
    cap = 2 * T // E
    cap_pad = -(-cap // 16) * 16
    R = min(E, 8)
    vmem = pl.BlockSpec(memory_space=pltpu.VMEM)
    hbm = pl.BlockSpec(memory_space=pl.ANY)
    dma = pltpu.SemaphoreType.DMA
    weights = (w_gate, w_up, w_down)
    weight_shapes = [jax.ShapeDtypeStruct(w.shape, BF16) for w in weights]
    summed, *swapped = pl.pallas_call(
        functools.partial(kernel, E, cap_pad, R),
        out_shape=[jax.ShapeDtypeStruct((T, F), BF16)] + weight_shapes,
        in_specs=[hbm, vmem, vmem, hbm, hbm, hbm],
        out_specs=[vmem, hbm, hbm, hbm],
        scratch_shapes=[
            pltpu.VMEM((T, F), BF16),
            pltpu.VMEM((E, cap_pad, F), BF16),
            pltpu.VMEM((E, 4, cap_pad, F), BF16),
            pltpu.VMEM((4, F, 2 * H), BF16),
            pltpu.VMEM((4, H, F), BF16),
            pltpu.VMEM((E, 4, cap_pad, H), BF16),
            pltpu.VMEM((E, cap_pad, F), BF16),
            pltpu.VMEM((E * cap_pad, F), BF16),
            pltpu.VMEM((T, E * cap_pad), BF16),
            pltpu.VMEM((1, T), F32),
            pltpu.VMEM((T, 128), F32),
            pltpu.VMEM((cap_pad, 2 * H), F32),
            dma((1,)), dma((9,)), dma((3 * PIECES,)), dma((3 * PIECES,)), dma((3,)), dma((3,)),
            dma((E,)), dma((E,)), dma((E,)), dma((E,)),
            dma((2, R)), dma((2, R)), dma((2, R)), dma((2, R)), dma((3, R)), dma((3, R)),
        ],
        compiler_params=pltpu.CompilerParams(
            collective_id=0, has_side_effects=True, vmem_limit_bytes=56 * 2**20
        ),
    )(tokens, route_ids.T, route_scores.T, *weights)
    mixed_shape = jax.ShapeDtypeStruct((T, F), BF16)
    return tuple(pl.pallas_call(
        place_kernel,
        out_shape=[mixed_shape] + weight_shapes,
        in_specs=[pl.BlockSpec(memory_space=pltpu.SMEM)] + [hbm] * 7,
        out_specs=[hbm] * 4,
        scratch_shapes=[pltpu.VMEM((T, F), BF16)]
        + [pltpu.VMEM(w.shape, BF16) for w in weights]
        + [dma((3 * PIECES + 1,)), dma((3 * PIECES + 1,))],
        compiler_params=pltpu.CompilerParams(has_side_effects=True, vmem_limit_bytes=56 * 2**20),
    )(partner, summed, *weights, *swapped))


def solution(mesh):
    return jax.shard_map(
        body,
        mesh=mesh,
        in_specs=(
            P("expert", "dp"),
            P("expert", None),
            P("expert", None),
            P(),
            P("expert", None, "dp"),
            P("expert", None, "dp"),
            P("expert", "dp", None),
        ),
        out_specs=(
            P("expert", "dp"),
            P("expert", None, "dp"),
            P("expert", None, "dp"),
            P("expert", "dp", None),
        ),
        check_vma=False,
    )
```
